32 devices in a mesh: ctx: 8 (over z, y), tp: 4 (over x, core).
Axes of the slice: x: 2, y: 2, z: 4, core: 2. Of those that a mesh axis runs over, the one named last changes fastest.
Arguments:
- queries: bfloat16 [2048, 8192], P('ctx', 'tp'), may hold values from -6 to 6
- new_keys: bfloat16 [2048, 1024], P('ctx', 'tp'), may hold values from -6 to 6
- new_values: bfloat16 [2048, 1024], P('ctx', 'tp'), may hold values from -6 to 6
- positions: int32 [2048], P('ctx'), may hold values from 0 to 262143, as said below
- cache_keys: bfloat16 [16384, 1024], P('ctx', 'tp'), may hold values from -6 to 6
- cache_values: bfloat16 [16384, 1024], P('ctx', 'tp'), may hold values from -6 to 6
- pattern: int32 [32, 4], P('ctx'), may hold values from 0 to 7, all different within a row; in each aligned block of 4 rows (0 to 3, 4 to 7, ...) at most 2 rows name the same one
- out_weight: bfloat16 [8192, 8192], P('tp'), may hold values from -0.0625 to 0.0625
Outputs:
- mixed: bfloat16 [2048, 8192], P(('ctx', 'tp'))
The draws below stay inside these ranges and needn't reach their ends.
Inputs may be any that keep to these rules, and one draw needn't show every extreme that they name: All 2048 positions are distinct. `pattern`: each row names 4 different segments; among the 4 query blocks of one ctx device at most 2 name the same segment, and 2 do in some devices.
All inputs are finite; a program needn't handle non-finite values.
Results may differ from the reference program's by a relative error of at most 0.0075.
Values may be sent and summed in bfloat16 or wider, within the bound.
A program may use at most 128 MiB of HBM per device.

```python
import math
import jax
import jax.numpy as jnp
import numpy as np
from jax import lax

D = 8192
H = 64
KVH = 8
HD = 128
QB = 64
TOPB = 4
CAP = 2
SPAN = 262144
QB_DEV = 4
KV_DEV = 2048
NQB = 32
QTOK = 2048
CTXLEN = 16384
N_CTX = 8


def spread_positions(key):
    base_key = jax.random.fold_in(key, 7)
    order = jax.random.permutation(jax.random.fold_in(base_key, 1), QTOK).astype(jnp.int32)
    stride = SPAN // QTOK
    jitter = jax.random.randint(jax.random.fold_in(base_key, 2), (QTOK,), 0, stride, dtype=jnp.int32)
    jitter = jnp.where(order == 0, 0, jnp.where(order == QTOK - 1, stride - 1, jitter))
    return (order * stride + jitter).astype(jnp.int32)


def draw_positions(key, part):
    return spread_positions(key)


def draw_queries(key, part):
    own_key = jax.random.fold_in(key, 21)
    return jnp.clip(1.5 * jax.random.normal(own_key, (QTOK, H * HD), jnp.float32), -6.0, 6.0).astype(jnp.bfloat16)


def draw_new_keys(key, part):
    own_key = jax.random.fold_in(key, 22)
    return jnp.clip(jax.random.normal(own_key, (QTOK, KVH * HD), jnp.float32), -6.0, 6.0).astype(jnp.bfloat16)


def draw_cache_keys(key, part):
    own_key = jax.random.fold_in(key, 23)
    return jnp.clip(jax.random.normal(own_key, (CTXLEN, KVH * HD), jnp.float32), -6.0, 6.0).astype(jnp.bfloat16)


def block_levels(key, dims, pieces, smallest, top_value):
    def one(dim, shards_of):
        steps = jax.random.uniform(jax.random.fold_in(jax.random.fold_in(key, 6), dim), (shards_of,), jnp.float32, smallest / len(pieces), top_value / len(pieces))
        return jnp.repeat(jnp.exp(steps), dims[dim] // shards_of).reshape((-1,) + (1,) * (len(dims) - dim - 1))

    loudness = one(*pieces[0])
    for cut in pieces[1:]:
        loudness = loudness * one(*cut)
    return loudness


def routed_block(key, own, number, rows, number_of, top, most, skew):
    ranking = jax.random.permutation(key, number_of)
    heavy_load, common = portions_of(number_of, rows * top, most, skew, True), portions_of(number_of, rows * top, most, skew, False)
    places = jnp.arange(number_of)

    def named(sizes, rotation):
        used = int((sizes > 0).sum())
        fixed = max(1, used // 4)
        passed = fixed + (places - fixed + rotation * (used - fixed)) % max(1, number_of - fixed)
        return jnp.zeros((number_of,), jnp.int32).at[ranking[jnp.where(places < fixed, places, passed)]].set(jnp.asarray(sizes, jnp.int32))

    sizes = jnp.where(number % 4 == 0, named(heavy_load, number // 4), named(common, number - number // 4 - 1))
    mixed = jax.random.permutation(jax.random.fold_in(own, 3), number_of)
    source_of, sink = mixed[0:number_of // 2 * 2:2], mixed[1:number_of // 2 * 2:2]
    margin = jnp.minimum(sizes[source_of] - 1, most - sizes[sink]) // 2
    margin = jnp.where((source_of == ranking[0]) | (sink == ranking[0]) | (sizes[sink] == 0), 0, jnp.maximum(margin, 0))
    passed = jax.random.randint(jax.random.fold_in(own, 4), (number_of // 2,), 0, 1 << 20) % (margin + 1)
    sizes = sizes.at[source_of].add(-passed).at[sink].add(passed)
    labels = jnp.searchsorted(jnp.cumsum(sizes), jnp.arange(rows * top), side="right").astype(jnp.int32)
    grid = labels.reshape(top, rows).T
    grid = grid[jax.random.permutation(jax.random.fold_in(own, 1), rows)]
    rotation = jax.random.randint(jax.random.fold_in(own, 2), (rows, 1), 0, top)
    return jnp.take_along_axis(grid, (jnp.arange(top)[None, :] + rotation) % top, axis=1)


def portions_of(number_of, total, limit, slope, full):
    loads = [(1 << 20) // math.isqrt(rank ** slope) + 1 for rank in range(1, number_of + 1)]
    largest = limit if full else min(limit, max(-(-total // number_of), total * loads[0] // sum(loads)))
    least = 1 if total - largest >= number_of - 1 else 0
    counts, spare = [largest] + [least] * (number_of - 1), total - largest - least * (number_of - 1)
    while spare > 0:
        movable = [i for i in range(1, number_of) if counts[i] < largest] or [i for i in range(1, number_of) if counts[i] < limit]
        whole, remaining = sum([loads[i] for i in movable]), spare
        for i in movable:
            addition = min(limit - counts[i], max(1, remaining * loads[i] // whole), spare)
            counts[i] = counts[i] + addition
            spare = spare - addition
    return np.array(counts)


def gaussian(key, shape, width, most, pieces=(), held_as=jnp.bfloat16):
    factor_of = block_levels(key, shape, pieces, -0.22, 0.18) if pieces else 1.0
    result = jax.random.normal(key, shape, jnp.float32) * width * factor_of
    return jnp.minimum(jnp.maximum(result, -most), most).astype(held_as)


def setup_inputs(seed: int = 0) -> dict:
    splits = jax.random.split(jax.random.key(seed), 9)
    queries = draw_queries(jax.random.fold_in(splits[8], 71), 0)
    new_keys = draw_new_keys(jax.random.fold_in(splits[8], 71), 0)
    new_values = gaussian(splits[2], (QTOK, KVH * HD), 1.0, 6.0, ((0, 8), (1, 4)))
    positions = draw_positions(jax.random.fold_in(splits[8], 71), 0)
    cache_keys = draw_cache_keys(jax.random.fold_in(splits[8], 71), 0)
    cache_values = gaussian(splits[5], (CTXLEN, KVH * HD), 1.0, 6.0, ((0, 8), (1, 4)))
    pattern_keys = jax.random.split(jax.random.fold_in(splits[6], 1), NQB // QB_DEV)
    pattern_turns = jax.random.permutation(jax.random.fold_in(splits[6], 3), NQB // QB_DEV)
    pattern = jax.vmap(lambda own, number: routed_block(jax.random.fold_in(splits[6], 2), own, number, QB_DEV, N_CTX, TOPB, CAP, 2))(pattern_keys, pattern_turns).reshape((NQB, TOPB))
    out_weight = gaussian(splits[7], (H * HD, D), (H * HD) ** -0.5, 0.0625, ((0, 4),))
    return {"queries": queries, "new_keys": new_keys, "new_values": new_values, "positions": positions, "cache_keys": cache_keys, "cache_values": cache_values, "pattern": pattern, "out_weight": out_weight}


NEG_FILL = -1e+30

def reference(queries, new_keys, new_values, positions, cache_keys, cache_values, pattern, out_weight):
    group_size = H // KVH
    scaling = 1.0 / math.sqrt(HD)
    segment_keys = cache_keys.reshape(N_CTX, KV_DEV, KVH, HD)
    segment_values = cache_values.reshape(N_CTX, KV_DEV, KVH, HD)
    fresh_keys = new_keys.reshape(QTOK, KVH, HD).astype(jnp.float32)
    fresh_values = new_values.reshape(QTOK, KVH, HD).astype(jnp.float32)
    block_positions = positions.reshape(NQB, QB)

    def one_block(inputs):
        block_queries, block_pattern, query_positions = inputs
        query_float = block_queries.reshape(QB, KVH, group_size, HD).astype(jnp.float32)

        def one_segment(segment):
            seg_keys = lax.dynamic_index_in_dim(segment_keys, segment, 0, keepdims=False).astype(jnp.float32)
            seg_values = lax.dynamic_index_in_dim(segment_values, segment, 0, keepdims=False).astype(jnp.float32)
            scores = jnp.einsum('tgrd,sgd->tgrs', query_float, seg_keys) * scaling
            largest = lax.optimization_barrier(jnp.max(scores, axis=-1))
            weights = jnp.exp(scores - largest[..., None])
            totals = lax.optimization_barrier(jnp.sum(weights, axis=-1))
            rounded = lax.optimization_barrier(weights.astype(jnp.bfloat16)).astype(jnp.float32)
            mixed_values = jnp.einsum('tgrs,sgd->tgrd', rounded, seg_values) / totals[..., None]
            return (mixed_values, largest + jnp.log(totals))
        part_out, part_log = lax.map(one_segment, block_pattern)
        scores = jnp.einsum('tgrd,sgd->tgrs', query_float, fresh_keys) * scaling
        visible = (positions[None, :] <= query_positions[:, None])[:, None, None, :]
        masked = jnp.where(visible, scores, NEG_FILL)
        largest = lax.optimization_barrier(jnp.max(masked, axis=-1))
        weights = jnp.where(visible, jnp.exp(masked - largest[..., None]), 0.0)
        totals = lax.optimization_barrier(jnp.sum(weights, axis=-1))
        rounded = lax.optimization_barrier(weights.astype(jnp.bfloat16)).astype(jnp.float32)
        fresh_out = jnp.einsum('tgrs,sgd->tgrd', rounded, fresh_values) / totals[..., None]
        fresh_log = largest + jnp.log(totals)
        all_log = jnp.concatenate([part_log, fresh_log[None]], axis=0)
        all_out = jnp.concatenate([part_out, fresh_out[None]], axis=0)
        top_log = lax.optimization_barrier(jnp.max(all_log, axis=0))
        log_total = top_log + jnp.log(lax.optimization_barrier(jnp.sum(jnp.exp(all_log - top_log[None]), axis=0)))
        shares = jnp.exp(all_log - log_total[None])
        attended = lax.optimization_barrier(jnp.sum(shares[..., None] * all_out, axis=0))
        return attended.reshape(QB, H * HD).astype(jnp.bfloat16)
    attention = lax.map(one_block, (queries.reshape(NQB, QB, H * HD), pattern, block_positions))
    attention = attention.reshape(QTOK, H * HD)
    return jnp.dot(attention, out_weight, preferred_element_type=jnp.float32).astype(jnp.bfloat16)
```

```python
import functools
import math

import jax
import jax.numpy as jnp
from jax import lax
from jax.experimental import pallas as pl
from jax.experimental.pallas import tpu as pltpu
from jax.sharding import PartitionSpec as P

H = 64
KVH = 8
HD = 128
TOPB = 4
CAP = 2
ROWS = 256
NEG_FILL = -1e30
LOG2E = math.log2(math.e)
SCALE2 = LOG2E / math.sqrt(HD)


def nt_dot(a, b):
    return lax.dot_general(a, b, (((1,), (1,)), ((), ())), preferred_element_type=jnp.float32)


def attention_kernel(
    n, q_ref, k_ref, v_ref, fresh_ref, meta_ref, column_ref, slot_ref, out_ref,
    q_all, meta_all, fr_all, kk, vv, fk, fv, bias, qsel, o_out, o_in, l_out, l_in, fo, fl,
    local_sem, kv_send, kv_recv, q_send, q_recv, m_send, m_recv, f_send, f_recv,
    mp_send, fp_send, o_send, o_recv, l_send, l_recv,
):
    planes = n // 2
    tokens = q_ref.shape[0]
    heads = q_ref.shape[1] // HD
    groups = k_ref.shape[1] // HD
    per_group = heads // groups
    block = tokens // 4
    me = lax.axis_index("ctx")
    par = lax.rem(me, 2)
    here = lax.div(me, 2)
    mate = me + 1 - 2 * par

    def column(plane):
        return {"ctx": 2 * plane + par}

    barrier = pltpu.get_barrier_semaphore()
    for step in range(1, planes):
        pl.semaphore_signal(
            barrier, inc=1, device_id=column(lax.rem(here + step, planes)),
            device_id_type=pl.DeviceIdType.MESH,
        )
    pl.semaphore_signal(
        barrier, inc=1, device_id={"ctx": mate}, device_id_type=pl.DeviceIdType.MESH
    )
    pl.semaphore_wait(barrier, planes)

    def remote(src, dst, send, recv, target):
        return pltpu.make_async_remote_copy(
            src_ref=src, dst_ref=dst, send_sem=send, recv_sem=recv, device_id=target,
            device_id_type=pl.DeviceIdType.MESH,
        )

    def chain(kind, s, side):
        target = column(s if side is None else here + 1 if side else here - 1)
        side = side or 0
        if kind == "q":
            return remote(q_all.at[s], q_all.at[s], q_send.at[side, s], q_recv.at[s], target)
        g = 2 * s + par
        if kind == "m":
            return remote(meta_all.at[g], meta_all.at[g], m_send.at[side, s], m_recv.at[g], target)
        return remote(fr_all.at[g], fr_all.at[g], f_send.at[side, s], f_recv.at[g], target)

    def to_mate(kind, s):
        g = 2 * s + par
        if kind == "m":
            return remote(meta_all.at[g], meta_all.at[g], mp_send.at[s], m_recv.at[g], {"ctx": mate})
        return remote(fr_all.at[g], fr_all.at[g], fp_send.at[s], f_recv.at[g], {"ctx": mate})

    def on_sides(s, act):
        @pl.when(jnp.logical_and(s <= here, here + 1 < planes))
        def _():
            act(1)

        @pl.when(jnp.logical_and(s >= here, here >= 1))
        def _():
            act(0)

    locals_ = [
        pltpu.make_async_copy(meta_ref, meta_all.at[me], local_sem.at[0]),
        pltpu.make_async_copy(q_ref, q_all.at[here], local_sem.at[1]),
        pltpu.make_async_copy(fresh_ref, fr_all.at[me], local_sem.at[2]),
    ]
    kv_copies = []
    for g in range(groups):
        cols = pl.ds(g * HD, HD)
        locals_.append(
            pltpu.make_async_copy(k_ref.at[:, cols], kk.at[par, g], local_sem.at[3 + 2 * g])
        )
        locals_.append(
            pltpu.make_async_copy(
                v_ref.at[:, cols], vv.at[par, g, :, pl.ds(0, HD)], local_sem.at[4 + 2 * g]
            )
        )
        kv_copies.append(
            remote(k_ref.at[:, cols], kk.at[par, g], kv_send.at[2 * g], kv_recv.at[2 * g],
                   {"ctx": mate})
        )
        kv_copies.append(
            remote(v_ref.at[:, cols], vv.at[par, g, :, pl.ds(0, HD)], kv_send.at[2 * g + 1],
                   kv_recv.at[2 * g + 1], {"ctx": mate})
        )
    for c in locals_:
        c.start()
    for c in locals_[:3]:
        c.wait()
    for kind in ("m", "q", "f"):
        on_sides(here, lambda side, kind=kind: chain(kind, here, side).start())
    to_mate("m", here).start()
    to_mate("f", here).start()
    for c in kv_copies:
        c.start()
    ones = jnp.ones((vv.shape[2], HD), jnp.bfloat16)
    for e in range(2):
        for g in range(groups):
            vv[e, g, :, HD:] = ones
    for c in locals_[3:]:
        c.wait()

    def soft(scores):
        top = jnp.max(scores, axis=1, keepdims=True)
        return top, jnp.exp2(scores - top).astype(jnp.bfloat16)

    def choose(s, e):
        g = 2 * s + par
        for r in range(CAP):
            row = (2 * here + e) * CAP + r
            which = meta_all[g, pl.ds(row, 1), :][:, :HD]
            marks = [jnp.broadcast_to(which, (block, HD)) == b for b in range(3)]
            for h in range(heads):
                cut = [
                    q_all[s, b * block:(b + 1) * block, h * HD:(h + 1) * HD].astype(jnp.float32)
                    for b in range(4)
                ]
                got = jnp.where(
                    marks[0], cut[0],
                    jnp.where(marks[1], cut[1], jnp.where(marks[2], cut[2], cut[3])),
                )
                qsel[h, r * block:(r + 1) * block, :] = got.astype(jnp.bfloat16)

    def work(s, e, outs, logs):
        choose(s, e)
        span = 2 * block

        def step(i, carry):
            g = lax.div(i, per_group // 2)
            q = qsel[pl.ds(2 * i, 2)].reshape(2 * span, HD)
            scores = nt_dot(q, kk[e, g]) * SCALE2
            top, weights = soft(scores)
            both = jnp.dot(weights, vv[e, g], preferred_element_type=jnp.float32)
            total = both[:, HD:]
            result = both[:, :HD] / total
            log = top + jnp.log2(total)
            for j in range(2):
                h = 2 * i + j
                lanes = pl.ds(pl.multiple_of(h * HD, HD), HD)
                for r in range(CAP):
                    a = j * span + r * block
                    outs[s, e, r, :, lanes] = result[a:a + block].astype(jnp.bfloat16)
                    logs[s, e, r, pl.ds(h, 1), pl.ds(0, block)] = log[a:a + block].T[:1]
            return carry

        lax.fori_loop(0, heads // 2, step, 0)

    def returns(s, e):
        return (
            remote(o_out.at[s, e], o_in.at[here, e], o_send.at[s, e], o_recv.at[here, e], column(s)),
            remote(l_out.at[s, e], l_in.at[here, e], l_send.at[s, e], l_recv.at[here, e], column(s)),
        )

    def others(act):
        def at_distance(k, carry):
            @pl.when(here - k >= 0)
            def _():
                act(here - k)

            @pl.when(here + k < planes)
            def _():
                act(here + k)

            return carry

        lax.fori_loop(1, planes, at_distance, 0)

    work(here, par, o_in, l_in)

    def first_half(s):
        for kind in ("m", "q", "f"):
            chain(kind, s, None).wait_recv()
            on_sides(s, lambda side, kind=kind: chain(kind, s, side).start())
            if kind != "q":
                to_mate(kind, s).start()
        work(s, par, o_out, l_out)
        for c in returns(s, par):
            c.start()

    others(first_half)
    for c in kv_copies:
        c.wait()

    def second_half(s):
        work(s, 1 - par, o_out, l_out)
        for c in returns(s, 1 - par):
            c.start()

    others(second_half)
    work(here, 1 - par, o_in, l_in)

    def from_mate(s, carry):
        g = 2 * s + 1 - par
        remote(meta_all.at[g], meta_all.at[g], mp_send.at[s], m_recv.at[g], {"ctx": mate}).wait_recv()
        remote(fr_all.at[g], fr_all.at[g], fp_send.at[s], f_recv.at[g], {"ctx": mate}).wait_recv()
        return carry

    lax.fori_loop(0, planes, from_mate, 0)
    mine = jnp.broadcast_to(column_ref[...], (tokens, tokens))
    for d in range(n):
        there = jnp.broadcast_to(meta_all[d, 2 * n:2 * n + 1, :], (tokens, tokens))
        bias[:, d * tokens:(d + 1) * tokens] = jnp.where(there <= mine, 0.0, NEG_FILL)
        for g in range(groups):
            rows = slice(d * tokens, (d + 1) * tokens)
            fk[g, rows, :] = fr_all[d, 0, :, g * HD:(g + 1) * HD]
            fv[g, rows, :HD] = fr_all[d, 1, :, g * HD:(g + 1) * HD]
    for g in range(groups):
        fv[g, :, HD:] = jnp.ones((n * tokens, HD), jnp.bfloat16)

    def fresh_head(h, carry):
        g = lax.div(h, per_group)
        lanes = pl.ds(pl.multiple_of(h * HD, HD), HD)
        scores = nt_dot(q_ref[:, lanes], fk[g]) * SCALE2 + bias[...]
        top, weights = soft(scores)
        both = jnp.dot(weights, fv[g], preferred_element_type=jnp.float32)
        total = both[:, HD:]
        fo[:, lanes] = both[:, :HD] / total
        fl[h] = top + jnp.log2(total)
        return carry

    lax.fori_loop(0, heads, fresh_head, 0)

    def arrived(s):
        for e in range(2):
            remote(o_out.at[s, e], o_in.at[s, e], o_send.at[s, e], o_recv.at[s, e], column(s)).wait_recv()
            remote(l_out.at[s, e], l_in.at[s, e], l_send.at[s, e], l_recv.at[s, e], column(s)).wait_recv()

    others(arrived)
    for b in range(4):
        rows = slice(b * block, (b + 1) * block)
        slots = [slot_ref[b * TOPB + j] for j in range(TOPB)]
        spots = [
            (lax.div(x, 4), lax.rem(lax.div(x, 2), 2), lax.rem(x, 2)) for x in slots
        ]
        tables = [l_in[p, e, r].T for p, e, r in spots]
        for h in range(heads):
            logs = [
                jnp.broadcast_to(t[:block, h:h + 1], (block, HD)) for t in tables
            ] + [fl[h, rows, :]]
            top = functools.reduce(jnp.maximum, logs)
            shares = [jnp.exp2(x - top) for x in logs]
            whole = functools.reduce(jnp.add, shares)
            lanes = slice(h * HD, (h + 1) * HD)
            mixed = shares[-1] * fo[rows, lanes]
            for (p, e, r), w in zip(spots, shares):
                mixed = mixed + w * o_in[p, e, r, :, lanes].astype(jnp.float32)
            out_ref[rows, lanes] = (mixed / whole).astype(out_ref.dtype)

    def sent(s, carry):
        on_sides(s, lambda side: [chain(kind, s, side).wait_send() for kind in ("m", "q", "f")])
        to_mate("m", s).wait_send()
        to_mate("f", s).wait_send()
        return carry

    lax.fori_loop(0, planes, sent, 0)

    def back(s):
        for e in range(2):
            for c in returns(s, e):
                c.wait_send()

    others(back)


def attend(n, queries, keys, values, fresh, meta, column, slots):
    planes = n // 2
    tokens, width = queries.shape
    heads = width // HD
    groups = keys.shape[1] // HD
    span = keys.shape[0]
    block = tokens // 4
    vmem = pl.BlockSpec(memory_space=pltpu.VMEM)
    bf, f32 = jnp.bfloat16, jnp.float32
    dma = pltpu.SemaphoreType.DMA
    return pl.pallas_call(
        functools.partial(attention_kernel, n),
        out_shape=jax.ShapeDtypeStruct((tokens, width), bf),
        in_specs=[vmem] * 6 + [pl.BlockSpec(memory_space=pltpu.SMEM)],
        out_specs=vmem,
        scratch_shapes=[
            pltpu.VMEM((planes, tokens, width), bf),
            pltpu.VMEM((n,) + meta.shape, jnp.int32),
            pltpu.VMEM((n,) + fresh.shape, bf),
            pltpu.VMEM((2, groups, span, HD), bf),
            pltpu.VMEM((2, groups, span, 2 * HD), bf),
            pltpu.VMEM((groups, n * tokens, HD), bf),
            pltpu.VMEM((groups, n * tokens, 2 * HD), bf),
            pltpu.VMEM((tokens, n * tokens), f32),
            pltpu.VMEM((heads, 2 * block, HD), bf),
            pltpu.VMEM((planes, 2, CAP, block, width), bf),
            pltpu.VMEM((planes, 2, CAP, block, width), bf),
            pltpu.VMEM((planes, 2, CAP, heads, HD), f32),
            pltpu.VMEM((planes, 2, CAP, heads, HD), f32),
            pltpu.VMEM((tokens, width), f32),
            pltpu.VMEM((heads, tokens, HD), f32),
            dma((3 + 2 * groups,)),
            dma((2 * groups,)),
            dma((2 * groups,)),
            dma((2, planes)),
            dma((planes,)),
            dma((2, planes)),
            dma((n,)),
            dma((2, planes)),
            dma((n,)),
            dma((planes,)),
            dma((planes,)),
            dma((planes, 2)),
            dma((planes, 2)),
            dma((planes, 2)),
            dma((planes, 2)),
        ],
        compiler_params=pltpu.CompilerParams(
            collective_id=0, has_side_effects=True, vmem_limit_bytes=62 * 1024 * 1024
        ),
    )(queries, keys, values, fresh, meta, column, slots)


def per_device(
    queries, new_keys, new_values, positions, cache_keys, cache_values, pattern, out_weight
):
    n = lax.axis_size("ctx")
    tokens = queries.shape[0]
    flat = pattern.reshape(-1)
    hits = (flat[:, None] == jnp.arange(n, dtype=jnp.int32)[None, :]).astype(jnp.int32)
    earlier = jnp.cumsum(hits, axis=0) - hits
    slots = flat * CAP + jnp.sum(earlier * hits, axis=1)
    owners = (slots[None, :] == jnp.arange(n * CAP, dtype=jnp.int32)[:, None]).astype(jnp.int32)
    blocks = jnp.sum(owners * (jnp.arange(flat.shape[0], dtype=jnp.int32) // TOPB)[None, :], axis=1)
    meta = jnp.concatenate(
        [
            jnp.broadcast_to(blocks[:, None], (n * CAP, tokens)),
            jnp.broadcast_to(positions[None, :], (8, tokens)),
        ],
        axis=0,
    )
    fresh = jnp.stack([new_keys, new_values])
    attention = attend(
        n, queries, cache_keys, cache_values, fresh, meta, positions.reshape(tokens, 1), slots
    )
    part = jnp.dot(attention, out_weight, preferred_element_type=jnp.float32).astype(jnp.bfloat16)
    return lax.psum_scatter(part, "tp", scatter_dimension=0, tiled=True)


def solution(mesh):
    placed = (
        P("ctx", "tp"),
        P("ctx", "tp"),
        P("ctx", "tp"),
        P("ctx"),
        P("ctx", "tp"),
        P("ctx", "tp"),
        P("ctx", None),
        P("tp", None),
    )
    return jax.shard_map(
        per_device, mesh=mesh, in_specs=placed, out_specs=P(("ctx", "tp"), None), check_vma=False
    )
```

```python
import functools
import math

import jax
import jax.numpy as jnp
from jax import lax
from jax.experimental import pallas as pl
from jax.experimental.pallas import tpu as pltpu
from jax.sharding import PartitionSpec as P

H = 64
KVH = 8
HD = 128
TOPB = 4
CAP = 2
ROWS = 256
NEG_FILL = -1e30
LOG2E = math.log2(math.e)
SCALE2 = LOG2E / math.sqrt(HD)


def nt_dot(a, b):
    return lax.dot_general(a, b, (((1,), (1,)), ((), ())), preferred_element_type=jnp.float32)


def attention_kernel(
    n, q_ref, k_ref, v_ref, fresh_ref, meta_ref, column_ref, slot_ref, out_ref,
    q_all, meta_all, fr_all, kk, vv, fk, fv, bias, qsel, o_out, o_in, l_out, l_in, fo, fl,
    *rest,
):
    (local_sem, kv_send, kv_recv, q_send, q_recv, m_send, m_recv, f_send, f_recv,
     mp_send, fp_send, o_send, o_recv, l_send, l_recv) = rest[-15:]
    held_a, held_b, fheld_a, fheld_b = (rest[0], rest[1], rest[0], rest[1])
    if n * q_ref.shape[0] != k_ref.shape[0]:
        fheld_a, fheld_b = rest[2], rest[3]
    planes = n // 2
    tokens = q_ref.shape[0]
    heads = q_ref.shape[1] // HD
    groups = k_ref.shape[1] // HD
    per_group = heads // groups
    block = tokens // 4
    me = lax.axis_index("ctx")
    par = lax.rem(me, 2)
    here = lax.div(me, 2)
    mate = me + 1 - 2 * par

    def column(plane):
        return {"ctx": 2 * plane + par}

    barrier = pltpu.get_barrier_semaphore()
    for step in range(1, planes):
        pl.semaphore_signal(
            barrier, inc=1, device_id=column(lax.rem(here + step, planes)),
            device_id_type=pl.DeviceIdType.MESH,
        )
    pl.semaphore_signal(
        barrier, inc=1, device_id={"ctx": mate}, device_id_type=pl.DeviceIdType.MESH
    )
    pl.semaphore_wait(barrier, planes)

    def remote(src, dst, send, recv, target):
        return pltpu.make_async_remote_copy(
            src_ref=src, dst_ref=dst, send_sem=send, recv_sem=recv, device_id=target,
            device_id_type=pl.DeviceIdType.MESH,
        )

    def chain(kind, s, side):
        target = column(s if side is None else here + 1 if side else here - 1)
        side = side or 0
        if kind == "q":
            return remote(q_all.at[s], q_all.at[s], q_send.at[side, s], q_recv.at[s], target)
        g = 2 * s + par
        if kind == "m":
            return remote(meta_all.at[g], meta_all.at[g], m_send.at[side, s], m_recv.at[g], target)
        return remote(fr_all.at[g], fr_all.at[g], f_send.at[side, s], f_recv.at[g], target)

    def to_mate(kind, s):
        g = 2 * s + par
        if kind == "m":
            return remote(meta_all.at[g], meta_all.at[g], mp_send.at[s], m_recv.at[g], {"ctx": mate})
        return remote(fr_all.at[g], fr_all.at[g], fp_send.at[s], f_recv.at[g], {"ctx": mate})

    def on_sides(s, act):
        @pl.when(jnp.logical_and(s <= here, here + 1 < planes))
        def _():
            act(1)

        @pl.when(jnp.logical_and(s >= here, here >= 1))
        def _():
            act(0)

    locals_ = [
        pltpu.make_async_copy(meta_ref, meta_all.at[me], local_sem.at[0]),
        pltpu.make_async_copy(q_ref, q_all.at[here], local_sem.at[1]),
        pltpu.make_async_copy(fresh_ref, fr_all.at[me], local_sem.at[2]),
    ]
    kv_copies = []
    for g in range(groups):
        cols = pl.ds(g * HD, HD)
        locals_.append(
            pltpu.make_async_copy(k_ref.at[:, cols], kk.at[par, g], local_sem.at[3 + 2 * g])
        )
        locals_.append(
            pltpu.make_async_copy(
                v_ref.at[:, cols], vv.at[par, g, :, pl.ds(0, HD)], local_sem.at[4 + 2 * g]
            )
        )
        kv_copies.append(
            remote(k_ref.at[:, cols], kk.at[par, g], kv_send.at[2 * g], kv_recv.at[2 * g],
                   {"ctx": mate})
        )
        kv_copies.append(
            remote(v_ref.at[:, cols], vv.at[par, g, :, pl.ds(0, HD)], kv_send.at[2 * g + 1],
                   kv_recv.at[2 * g + 1], {"ctx": mate})
        )
    for c in locals_:
        c.start()
    for c in locals_[:3]:
        c.wait()
    for kind in ("m", "q", "f"):
        on_sides(here, lambda side, kind=kind: chain(kind, here, side).start())
    to_mate("m", here).start()
    to_mate("f", here).start()
    for c in kv_copies:
        c.start()
    ones = jnp.ones((vv.shape[2], HD), jnp.bfloat16)
    for e in range(2):
        for g in range(groups):
            vv[e, g, :, HD:] = ones
    for c in locals_[3:]:
        c.wait()

    def choose(s, e):
        g = 2 * s + par
        for r in range(CAP):
            row = (2 * here + e) * CAP + r
            which = meta_all[g, pl.ds(row, 1), :][:, :HD]
            marks = [jnp.broadcast_to(which, (block, HD)) == b for b in range(3)]
            for h in range(heads):
                cut = [
                    q_all[s, b * block:(b + 1) * block, h * HD:(h + 1) * HD].astype(jnp.float32)
                    for b in range(4)
                ]
                got = jnp.where(
                    marks[0], cut[0],
                    jnp.where(marks[1], cut[1], jnp.where(marks[2], cut[2], cut[3])),
                )
                qsel[h, r * block:(r + 1) * block, :] = got.astype(jnp.bfloat16)

    def work(s, e, outs, logs):
        choose(s, e)
        span = 2 * block
        steps = heads // 2

        def score(i, held):
            g = lax.div(i, per_group // 2)
            scores = nt_dot(qsel[pl.ds(2 * i, 2)].reshape(2 * span, HD), kk[e, g])
            held[...] = scores
            return jnp.max(scores, axis=1, keepdims=True)

        def finish(i, held, top):
            g = lax.div(i, per_group // 2)
            weights = jnp.exp2((held[...] - top) * SCALE2).astype(jnp.bfloat16)
            both = jnp.dot(weights, vv[e, g], preferred_element_type=jnp.float32)
            total = both[:, HD:]
            result = both[:, :HD] / total
            log = top * SCALE2 + jnp.log2(total)
            for j in range(2):
                h = 2 * i + j
                lanes = pl.ds(pl.multiple_of(h * HD, HD), HD)
                for r in range(CAP):
                    a = j * span + r * block
                    outs[s, e, r, :, lanes] = result[a:a + block].astype(jnp.bfloat16)
                    logs[s, e, r, pl.ds(h, 1), pl.ds(0, block)] = log[a:a + block].T[:1]

        def step(j, top):
            later = score(2 * j + 1, held_b)
            finish(2 * j, held_a, top)
            top = score(jnp.minimum(2 * j + 2, steps - 1), held_a)
            finish(2 * j + 1, held_b, later)
            return top

        lax.fori_loop(0, steps // 2, step, score(0, held_a))

    def returns(s, e):
        return (
            remote(o_out.at[s, e], o_in.at[here, e], o_send.at[s, e], o_recv.at[here, e], column(s)),
            remote(l_out.at[s, e], l_in.at[here, e], l_send.at[s, e], l_recv.at[here, e], column(s)),
        )

    def others(*acts):
        def at_distance(k, carry):
            for act in acts:
                @pl.when(here - k >= 0)
                def _():
                    act(here - k)

                @pl.when(here + k < planes)
                def _():
                    act(here + k)

            return carry

        lax.fori_loop(1, planes, at_distance, 0)

    work(here, par, o_in, l_in)

    def pass_on(s):
        for kind in ("m", "q", "f"):
            chain(kind, s, None).wait_recv()
            on_sides(s, lambda side, kind=kind: chain(kind, s, side).start())
            if kind != "q":
                to_mate(kind, s).start()

    def first_half(s):
        work(s, par, o_out, l_out)
        for c in returns(s, par):
            c.start()

    others(pass_on, first_half)
    for c in kv_copies:
        c.wait()

    def second_half(s):
        work(s, 1 - par, o_out, l_out)
        for c in returns(s, 1 - par):
            c.start()

    others(second_half)
    work(here, 1 - par, o_in, l_in)

    def from_mate(s, carry):
        g = 2 * s + 1 - par
        remote(meta_all.at[g], meta_all.at[g], mp_send.at[s], m_recv.at[g], {"ctx": mate}).wait_recv()
        remote(fr_all.at[g], fr_all.at[g], fp_send.at[s], f_recv.at[g], {"ctx": mate}).wait_recv()
        return carry

    lax.fori_loop(0, planes, from_mate, 0)
    mine = jnp.broadcast_to(column_ref[...], (tokens, tokens))
    for d in range(n):
        there = jnp.broadcast_to(meta_all[d, 2 * n:2 * n + 1, :], (tokens, tokens))
        bias[:, d * tokens:(d + 1) * tokens] = jnp.where(there <= mine, 0.0, NEG_FILL)
        for g in range(groups):
            rows = slice(d * tokens, (d + 1) * tokens)
            fk[g, rows, :] = fr_all[d, 0, :, g * HD:(g + 1) * HD]
            fv[g, rows, :HD] = fr_all[d, 1, :, g * HD:(g + 1) * HD]
    for g in range(groups):
        fv[g, :, HD:] = jnp.ones((n * tokens, HD), jnp.bfloat16)

    def fresh_score(h, held):
        g = lax.div(h, per_group)
        lanes = pl.ds(pl.multiple_of(h * HD, HD), HD)
        scores = nt_dot(q_ref[:, lanes], fk[g]) + bias[...]
        held[...] = scores
        return jnp.max(scores, axis=1, keepdims=True)

    def fresh_finish(h, held, top):
        g = lax.div(h, per_group)
        lanes = pl.ds(pl.multiple_of(h * HD, HD), HD)
        weights = jnp.exp2((held[...] - top) * SCALE2).astype(jnp.bfloat16)
        both = jnp.dot(weights, fv[g], preferred_element_type=jnp.float32)
        total = both[:, HD:]
        fo[:, lanes] = both[:, :HD] / total
        fl[h] = top * SCALE2 + jnp.log2(total)

    def fresh_step(j, top):
        later = fresh_score(2 * j + 1, fheld_b)
        fresh_finish(2 * j, fheld_a, top)
        top = fresh_score(jnp.minimum(2 * j + 2, heads - 1), fheld_a)
        fresh_finish(2 * j + 1, fheld_b, later)
        return top

    lax.fori_loop(0, heads // 2, fresh_step, fresh_score(0, fheld_a))

    def arrived(s):
        for e in range(2):
            remote(o_out.at[s, e], o_in.at[s, e], o_send.at[s, e], o_recv.at[s, e], column(s)).wait_recv()
            remote(l_out.at[s, e], l_in.at[s, e], l_send.at[s, e], l_recv.at[s, e], column(s)).wait_recv()

    others(arrived)
    for b in range(4):
        rows = slice(b * block, (b + 1) * block)
        slots = [slot_ref[b * TOPB + j] for j in range(TOPB)]
        spots = [
            (lax.div(x, 4), lax.rem(lax.div(x, 2), 2), lax.rem(x, 2)) for x in slots
        ]
        tables = [l_in[p, e, r].T for p, e, r in spots]
        for h in range(heads):
            logs = [
                jnp.broadcast_to(t[:block, h:h + 1], (block, HD)) for t in tables
            ] + [fl[h, rows, :]]
            top = functools.reduce(jnp.maximum, logs)
            shares = [jnp.exp2(x - top) for x in logs]
            whole = functools.reduce(jnp.add, shares)
            lanes = slice(h * HD, (h + 1) * HD)
            mixed = shares[-1] * fo[rows, lanes]
            for (p, e, r), w in zip(spots, shares):
                mixed = mixed + w * o_in[p, e, r, :, lanes].astype(jnp.float32)
            out_ref[rows, lanes] = (mixed / whole).astype(out_ref.dtype)

    def sent(s, carry):
        on_sides(s, lambda side: [chain(kind, s, side).wait_send() for kind in ("m", "q", "f")])
        to_mate("m", s).wait_send()
        to_mate("f", s).wait_send()
        return carry

    lax.fori_loop(0, planes, sent, 0)

    def back(s):
        for e in range(2):
            for c in returns(s, e):
                c.wait_send()

    others(back)


def attend(n, queries, keys, values, fresh, meta, column, slots):
    planes = n // 2
    tokens, width = queries.shape
    heads = width // HD
    groups = keys.shape[1] // HD
    span = keys.shape[0]
    block = tokens // 4
    vmem = pl.BlockSpec(memory_space=pltpu.VMEM)
    bf, f32 = jnp.bfloat16, jnp.float32
    dma = pltpu.SemaphoreType.DMA
    held = [pltpu.VMEM((tokens, span), f32)] * 2
    if n * tokens != span:
        held += [pltpu.VMEM((tokens, n * tokens), f32)] * 2
    return pl.pallas_call(
        functools.partial(attention_kernel, n),
        out_shape=jax.ShapeDtypeStruct((tokens, width), bf),
        in_specs=[vmem] * 6 + [pl.BlockSpec(memory_space=pltpu.SMEM)],
        out_specs=vmem,
        scratch_shapes=[
            pltpu.VMEM((planes, tokens, width), bf),
            pltpu.VMEM((n,) + meta.shape, jnp.int32),
            pltpu.VMEM((n,) + fresh.shape, bf),
            pltpu.VMEM((2, groups, span, HD), bf),
            pltpu.VMEM((2, groups, span, 2 * HD), bf),
            pltpu.VMEM((groups, n * tokens, HD), bf),
            pltpu.VMEM((groups, n * tokens, 2 * HD), bf),
            pltpu.VMEM((tokens, n * tokens), f32),
            pltpu.VMEM((heads, 2 * block, HD), bf),
            pltpu.VMEM((planes, 2, CAP, block, width), bf),
            pltpu.VMEM((planes, 2, CAP, block, width), bf),
            pltpu.VMEM((planes, 2, CAP, heads, HD), f32),
            pltpu.VMEM((planes, 2, CAP, heads, HD), f32),
            pltpu.VMEM((tokens, width), f32),
            pltpu.VMEM((heads, tokens, HD), f32),
            *held,
            dma((3 + 2 * groups,)),
            dma((2 * groups,)),
            dma((2 * groups,)),
            dma((2, planes)),
            dma((planes,)),
            dma((2, planes)),
            dma((n,)),
            dma((2, planes)),
            dma((n,)),
            dma((planes,)),
            dma((planes,)),
            dma((planes, 2)),
            dma((planes, 2)),
            dma((planes, 2)),
            dma((planes, 2)),
        ],
        compiler_params=pltpu.CompilerParams(
            collective_id=0, has_side_effects=True, vmem_limit_bytes=62 * 1024 * 1024
        ),
    )(queries, keys, values, fresh, meta, column, slots)


def project_kernel(nt, a_ref, w_ref, out_ref, a2, wbuf, part, own, mate_out, mate_in, x_out, x_in,
                   w_sem, mate_send, mate_recv, x_send, x_recv):
    pairs = nt // 2
    rows = a_ref.shape[0] // nt
    count, wide = own.shape[0], own.shape[2]
    me = lax.axis_index("tp")
    core = lax.rem(me, 2)
    x = lax.div(me, 2)
    mate = {"tp": me + 1 - 2 * core}

    def peer(d):
        return lax.rem(x + d, pairs)

    def fetch(j):
        return pltpu.make_async_copy(
            w_ref.at[:, pl.ds(pl.multiple_of(j * wide, wide), wide)],
            wbuf.at[lax.rem(j, 2)], w_sem.at[lax.rem(j, 2)],
        )

    fetch(0).start()
    fetch(1).start()
    barrier = pltpu.get_barrier_semaphore()
    for target in [mate] + [{"tp": 2 * peer(d) + core} for d in range(1, pairs)]:
        pl.semaphore_signal(
            barrier, inc=1, device_id=target, device_id_type=pl.DeviceIdType.MESH
        )
    pl.semaphore_wait(barrier, pairs)
    for t in range(nt):
        at = (t % 2) * pairs * rows + (t // 2) * rows
        a2[at:at + rows, :] = a_ref[t * rows:(t + 1) * rows, :]

    def swap(j):
        return pltpu.make_async_remote_copy(
            src_ref=mate_out.at[j], dst_ref=mate_in.at[j], send_sem=mate_send.at[j],
            recv_sem=mate_recv.at[j], device_id=mate, device_id_type=pl.DeviceIdType.MESH,
        )

    def across(j, d):
        return pltpu.make_async_remote_copy(
            src_ref=x_out.at[j, peer(d)], dst_ref=x_in.at[j, x], send_sem=x_send.at[j, d],
            recv_sem=x_recv.at[j, x], device_id={"tp": 2 * peer(d) + core},
            device_id_type=pl.DeviceIdType.MESH,
        )

    def arrival(j, d):
        return pltpu.make_async_remote_copy(
            src_ref=x_out.at[j, peer(d)], dst_ref=x_in.at[j, peer(d)], send_sem=x_send.at[j, d],
            recv_sem=x_recv.at[j, peer(d)], device_id={"tp": 2 * peer(d) + core},
            device_id_type=pl.DeviceIdType.MESH,
        )

    def add_mate(j):
        swap(j).wait_recv()
        total = own[j] + mate_in[j].astype(jnp.float32)
        own[j] = total
        for k in range(pairs):
            x_out[j, k] = total[k * rows:(k + 1) * rows].astype(jnp.bfloat16)
        for d in range(1, pairs):
            across(j, d).start()

    def step(j, carry):
        fetch(j).wait()
        part[...] = jnp.dot(
            a2[...], wbuf[lax.rem(j, 2)], preferred_element_type=jnp.float32
        ).reshape(part.shape)
        mate_out[j] = part[1 - core].astype(jnp.bfloat16)
        swap(j).start()
        own[j] = part[core]

        @pl.when(j + 2 < count)
        def _():
            fetch(j + 2).start()

        @pl.when(j >= 1)
        def _():
            add_mate(j - 1)

        return carry

    lax.fori_loop(0, count, step, 0)
    add_mate(count - 1)

    def last(j, carry):
        total = own[j, pl.ds(pl.multiple_of(x * rows, rows), rows), :]
        for d in range(1, pairs):
            arrival(j, d).wait_recv()
            total = total + x_in[j, peer(d)].astype(jnp.float32)
        out_ref[:, pl.ds(pl.multiple_of(j * wide, wide), wide)] = total.astype(out_ref.dtype)
        swap(j).wait_send()
        for d in range(1, pairs):
            across(j, d).wait_send()
        return carry

    lax.fori_loop(0, count, last, 0)


def project(nt, attention, out_weight):
    tokens, width = attention.shape
    columns = out_weight.shape[1]
    wide = 1024
    count = columns // wide
    pairs = nt // 2
    rows = tokens // nt
    bf, f32 = jnp.bfloat16, jnp.float32
    dma = pltpu.SemaphoreType.DMA
    return pl.pallas_call(
        functools.partial(project_kernel, nt),
        out_shape=jax.ShapeDtypeStruct((rows, columns), bf),
        in_specs=[pl.BlockSpec(memory_space=pltpu.VMEM), pl.BlockSpec(memory_space=pl.ANY)],
        out_specs=pl.BlockSpec(memory_space=pltpu.VMEM),
        scratch_shapes=[
            pltpu.VMEM((tokens, width), bf),
            pltpu.VMEM((2, width, wide), bf),
            pltpu.VMEM((2, tokens // 2, wide), f32),
            pltpu.VMEM((count, tokens // 2, wide), f32),
            pltpu.VMEM((count, tokens // 2, wide), bf),
            pltpu.VMEM((count, tokens // 2, wide), bf),
            pltpu.VMEM((count, pairs, rows, wide), bf),
            pltpu.VMEM((count, pairs, rows, wide), bf),
            dma((2,)),
            dma((count,)),
            dma((count,)),
            dma((count, pairs)),
            dma((count, pairs)),
        ],
        compiler_params=pltpu.CompilerParams(
            collective_id=1, has_side_effects=True, vmem_limit_bytes=48 * 1024 * 1024
        ),
    )(attention, out_weight)


def per_device(
    queries, new_keys, new_values, positions, cache_keys, cache_values, pattern, out_weight
):
    n = lax.axis_size("ctx")
    tokens = queries.shape[0]
    flat = pattern.reshape(-1)
    hits = (flat[:, None] == jnp.arange(n, dtype=jnp.int32)[None, :]).astype(jnp.int32)
    earlier = jnp.cumsum(hits, axis=0) - hits
    slots = flat * CAP + jnp.sum(earlier * hits, axis=1)
    owners = (slots[None, :] == jnp.arange(n * CAP, dtype=jnp.int32)[:, None]).astype(jnp.int32)
    blocks = jnp.sum(owners * (jnp.arange(flat.shape[0], dtype=jnp.int32) // TOPB)[None, :], axis=1)
    meta = jnp.concatenate(
        [
            jnp.broadcast_to(blocks[:, None], (n * CAP, tokens)),
            jnp.broadcast_to(positions[None, :], (8, tokens)),
        ],
        axis=0,
    )
    fresh = jnp.stack([new_keys, new_values])
    attention = attend(
        n, queries, cache_keys, cache_values, fresh, meta, positions.reshape(tokens, 1), slots
    )
    return project(lax.axis_size("tp"), attention, out_weight)


def solution(mesh):
    placed = (
        P("ctx", "tp"),
        P("ctx", "tp"),
        P("ctx", "tp"),
        P("ctx"),
        P("ctx", "tp"),
        P("ctx", "tp"),
        P("ctx", None),
        P("tp", None),
    )
    return jax.shard_map(
        per_device, mesh=mesh, in_specs=placed, out_specs=P(("ctx", "tp"), None), check_vma=False
    )
```
